512 devices in a mesh: replica: 16 (over x, z_hi, core), fsdp: 32 (over y, z_lo).
Axes of the slice: x: 4, y: 8, z: 8 (z_hi: 2, z_lo: 4; z = z_hi * 4 + z_lo), core: 2. Of those that a mesh axis runs over, the one named last changes fastest.
Arguments:
- local_weights: bfloat16 [16, 2048, 8192], P('replica', 'fsdp'), may hold values from -12 to 12
- global_weights: bfloat16 [2048, 8192], P('fsdp'), may hold values from -4 to 4
- momentum: float32 [2048, 8192], P('fsdp', 'replica'), may hold values from -1.5 to 1.5
Outputs:
- new_weights: bfloat16 [2048, 8192], P('fsdp')
- new_momentum: float32 [2048, 8192], P('fsdp', 'replica')
The draws below stay inside these ranges and needn't reach their ends.
All inputs are finite; a program needn't handle non-finite values. Where the reference program divides by a largest or mean magnitude, that divisor is 1e-20 or more.
Results may differ from the reference program's by a relative error of at most 0.007.
Values may be sent and summed in bfloat16 or wider, within the bound.
No kernel may reach another device: no remote copies, remote signals or barrier semaphores. Data moves between devices by JAX's collectives and lax.ppermute only.
A program may use at most 64 MiB of HBM per device.

```python
import jax
import jax.numpy as jnp
from jax import lax

D = 8192
ROWS_DEV = 64
GROUP = 64
NROWS = 2048
REPLICAS = 16


def shared_base(key):
    return jnp.clip(jax.random.normal(jax.random.fold_in(key, 101), (NROWS, D), jnp.float32), -4.0, 4.0)


def draw_global_weights(key, part):
    base = shared_base(key)
    return base.astype(jnp.bfloat16)


def draw_local_weights(key, part):
    base = shared_base(key)
    key = jax.random.fold_in(key, 7)
    row_pos = jnp.arange(NROWS, dtype=jnp.float32) / NROWS
    col_pos = jnp.arange(D, dtype=jnp.float32) / D
    row_draw = jax.random.uniform(jax.random.fold_in(key, 1), (NROWS,), jnp.float32)
    col_draw = jax.random.uniform(jax.random.fold_in(key, 2), (D,), jnp.float32)
    row_scale = 10.0 ** (0.5 * row_draw + 0.5 * row_pos)
    col_scale = 10.0 ** (0.5 * col_draw + 0.5 * col_pos)
    mix_draw = jax.random.uniform(jax.random.fold_in(key, 5), (NROWS // ROWS_DEV, REPLICAS), jnp.float32)
    mix_table = jnp.clip(2.0 * mix_draw - 0.5, 0.0, 1.0)
    mixing = jnp.repeat(jnp.repeat(mix_table, ROWS_DEV, axis=0), D // REPLICAS, axis=1)
    common = jnp.clip(jax.random.normal(jax.random.fold_in(key, 3), (1, NROWS, D), jnp.float32), -4.0, 4.0)
    own = jnp.clip(jax.random.normal(jax.random.fold_in(key, 4), (REPLICAS, NROWS, D), jnp.float32), -4.0, 4.0)
    noise = mixing[None] * common + (1.0 - mixing[None]) * own
    local = base[None] + 0.02 * row_scale[None, :, None] * col_scale[None, None, :] * noise
    return local.astype(jnp.bfloat16)


def steps_of(rng, dims, split, least, top_value):
    def one(axis_at, blocks):
        draws = jax.random.uniform(jax.random.fold_in(jax.random.fold_in(rng, 6), axis_at), (blocks,), jnp.float32, least / len(split), top_value / len(split))
        return jnp.repeat(jnp.exp(draws), dims[axis_at] // blocks).reshape((-1,) + (1,) * (len(dims) - axis_at - 1))

    loudness = one(*split[0])
    for cut in split[1:]:
        loudness = loudness * one(*cut)
    return loudness


def normal_values(stream_key, shape, scale, bound, cuts=(), kind=jnp.bfloat16):
    result = scale * jax.random.normal(stream_key, shape, jnp.float32)
    if cuts:
        result = result * steps_of(stream_key, shape, cuts, -0.22, 0.18)
    return jnp.clip(result, -bound, bound).astype(kind)


def setup_inputs(seed: int = 0) -> dict:
    seeds = jax.random.split(jax.random.key(seed), 4)
    return {
        "local_weights": draw_local_weights(jax.random.fold_in(seeds[3], 71), 0),
        "global_weights": draw_global_weights(jax.random.fold_in(seeds[3], 71), 0),
        "momentum": normal_values(seeds[2], (NROWS, D), 0.1, 1.5, ((0, 32), (1, 16)), jnp.float32),
    }


def group_codes(values):
    rows, cols = values.shape
    blocks = values.reshape(rows, cols // GROUP, GROUP)
    scale = (lax.optimization_barrier(jnp.max(jnp.abs(blocks), axis=2)) + 1e-06).astype(jnp.bfloat16)
    codes = (blocks / scale.astype(jnp.float32)[:, :, None]).astype(jnp.bfloat16)
    return (codes.reshape(rows, cols), scale)

def expand(codes, scale):
    rows, cols = codes.shape
    blocks = codes.reshape(rows, cols // GROUP, GROUP).astype(jnp.float32)
    return (blocks * scale.astype(jnp.float32)[:, :, None]).reshape(rows, cols)

def reference(local_weights, global_weights, momentum):
    base = global_weights.astype(jnp.float32)

    def accumulate(total, local_row):
        delta = local_row.astype(jnp.float32) - base
        codes, scale = group_codes(delta)
        return (total + expand(codes, scale), None)
    total, _ = lax.scan(accumulate, jnp.zeros((NROWS, D), jnp.float32), local_weights)
    average = total / REPLICAS
    spread = jnp.sqrt(jnp.sum(average * average) / (NROWS * D) + 1e-06)
    factor = jnp.minimum(1.0, 0.04 / spread)
    clipped = factor * average
    new_momentum = 0.9 * momentum + clipped
    update = 0.7 * (clipped + 0.9 * new_momentum)
    update_codes, update_scale = group_codes(update)
    new_weights = (base - expand(update_codes, update_scale)).astype(jnp.bfloat16)
    return (new_weights, new_momentum)
```

```python
import jax
import jax.numpy as jnp
from jax import lax
from jax.experimental import pallas as pl
from jax.experimental.pallas import tpu as pltpu
from jax.sharding import Mesh, PartitionSpec as P

NX, NZ, NC, NY, NL = 4, 2, 2, 8, 4
REPLICAS = NX * NZ * NC
AXES = ("x", "zh", "c", "y", "zl")
REPLICA = ("x", "zh", "c")
FSDP = ("y", "zl")
OWN = 512
PAIR = NZ * OWN
F32, BF16 = jnp.float32, jnp.bfloat16
VMEM = pl.BlockSpec(memory_space=pltpu.VMEM)
SMEM = pl.BlockSpec(memory_space=pltpu.SMEM)


def block_cols(x, h, core):
    return pl.ds(pl.multiple_of(((x * NZ + h) * NC + core) * OWN, OWN), OWN)


def delta_kernel(flip, core_ref, *refs):
    out_ref = refs[-1]
    for h in range(NZ):
        delta = refs[h][0].astype(F32) - refs[NZ + h][...].astype(F32)
        out_ref[0, :, h * OWN:(h + 1) * OWN] = delta.astype(BF16)


def delta_half(core, local, base, name):
    rows = base.shape[0]

    def cols(h, lead):
        def index(i, s):
            return lead + (0, (i * NZ + h) * NC + s[0])
        return index

    return pl.pallas_call(
        lambda *refs: delta_kernel(None, *refs),
        grid_spec=pltpu.PrefetchScalarGridSpec(
            num_scalar_prefetch=1,
            grid=(NX,),
            in_specs=[pl.BlockSpec((1, rows, OWN), cols(h, (0,))) for h in range(NZ)]
            + [pl.BlockSpec((rows, OWN), cols(h, ())) for h in range(NZ)],
            out_specs=pl.BlockSpec((1, rows, PAIR), lambda i, s: (i, 0, 0)),
        ),
        out_shape=jax.ShapeDtypeStruct((NX, rows, PAIR), BF16),
        cost_estimate=pl.CostEstimate(flops=rows * 4096, bytes_accessed=6 * rows * 4096, transcendentals=0),
        name=name,
    )(core, local, local, base, base)


def quad_kernel(parts_ref, mom_ref, out_ref):
    total = parts_ref[0].astype(F32)
    for k in range(1, NX):
        total = total + parts_ref[k].astype(F32)
    out_ref[:, :PAIR] = total.astype(BF16)
    out_ref[:, PAIR:] = mom_ref[...].astype(BF16)


def total_kernel(both_ref, out_ref):
    total = (both_ref[0, :, :PAIR].astype(F32) + both_ref[1, :, :PAIR].astype(F32)).astype(BF16)
    for k in range(NX):
        out_ref[k, :, :PAIR] = total
        for h in range(NZ):
            out_ref[k, :, PAIR + h * OWN:PAIR + (h + 1) * OWN] = both_ref[h, :, PAIR:]


def squares_kernel(own_ref, out_ref):
    acc = jnp.zeros((own_ref.shape[1], 128), F32)
    for k in range(NX):
        for j in range(PAIR // 128):
            part = own_ref[k, :, j * 128:(j + 1) * 128].astype(F32)
            acc = acc + part * part
    out_ref[...] = jnp.broadcast_to(jnp.sum(acc), out_ref.shape)


def final_kernel(entries, core_ref, half_ref, shares_ref, base_ref, mom_ref, own_ref, other_ref, new_ref, newmom_ref):
    core = core_ref[0]
    half = half_ref[0]
    total = jnp.sum(shares_ref[...]) / (REPLICAS * REPLICAS)
    spread = jnp.sqrt(total / entries + 1e-06)
    factor = jnp.minimum(1.0, 0.04 / spread) / REPLICAS

    def part(which, src_ref):
        for x in range(NX):
            for h in range(NZ):
                cols = block_cols(x, h, which)
                clipped = factor * src_ref[x, :, h * OWN:(h + 1) * OWN].astype(F32)
                mom = 0.9 * src_ref[x, :, PAIR + h * OWN:PAIR + (h + 1) * OWN].astype(F32) + clipped
                update = 0.7 * (clipped + 0.9 * mom)
                new_ref[:, cols] = (base_ref[:, cols].astype(F32) - update).astype(BF16)

    part(core, own_ref)
    part(1 - core, other_ref)
    x = half_ref[1]
    cols = pl.ds(pl.multiple_of(half * OWN, OWN), OWN)
    newmom_ref[...] = 0.9 * mom_ref[...] + factor * own_ref[x, :, cols].astype(F32)


def per_device(local_weights, global_weights, momentum):
    rows, width = global_weights.shape
    core = lax.axis_index("c").astype(jnp.int32)
    half = lax.axis_index("zh").astype(jnp.int32)
    xi = lax.axis_index("x").astype(jnp.int32)
    swap = [(0, 1), (1, 0)]
    send = delta_half((1 - core).reshape(1), local_weights, global_weights, "delta_send")
    keep = delta_half(core.reshape(1), local_weights, global_weights, "delta_keep")
    pair = keep.astype(F32) + lax.ppermute(send, "c", swap).astype(F32)
    parts = lax.all_to_all(pair.astype(BF16), "x", 0, 0, tiled=True)
    quad = pl.pallas_call(
        quad_kernel, in_specs=[VMEM] * 2, out_specs=VMEM,
        out_shape=jax.ShapeDtypeStruct((rows, PAIR + OWN), BF16), name="quad",
    )(parts, momentum)
    both = lax.all_gather(quad, "zh", axis=0)
    total = pl.pallas_call(
        total_kernel, in_specs=[VMEM], out_specs=VMEM,
        out_shape=jax.ShapeDtypeStruct((NX, rows, 2 * PAIR), BF16), name="total",
    )(both)
    own = lax.all_to_all(total, "x", 0, 0, tiled=True)
    other = lax.ppermute(own, "c", swap)
    group = NC * NY * NL
    squares = pl.pallas_call(
        squares_kernel, in_specs=[VMEM], out_specs=VMEM,
        out_shape=jax.ShapeDtypeStruct((group, 1), F32), name="squares",
    )(own)
    shares = lax.all_to_all(squares, ("c", "y", "zl"), 0, 0, tiled=True)
    entries = rows * width * NY * NL
    new_weights, new_momentum = pl.pallas_call(
        lambda *refs: final_kernel(entries, *refs),
        in_specs=[SMEM, SMEM] + [VMEM] * 5, out_specs=[VMEM, VMEM],
        out_shape=[jax.ShapeDtypeStruct((rows, width), BF16), jax.ShapeDtypeStruct(momentum.shape, F32)],
        name="final",
    )(core.reshape(1), jnp.stack([half, xi]), shares, global_weights, momentum, own, other)
    return (new_weights, new_momentum)


def solution(mesh):
    fine = Mesh(mesh.devices.reshape(NX, NZ, NC, NY, NL), AXES)
    in_specs = (P(REPLICA, FSDP, None), P(FSDP, None), P(FSDP, REPLICA))
    out_specs = (P(FSDP, None), P(FSDP, REPLICA))
    return jax.shard_map(
        per_device, mesh=fine, in_specs=in_specs, out_specs=out_specs, check_vma=False
    )
```

```python
import jax
import jax.numpy as jnp
from jax import lax
from jax.experimental import pallas as pl
from jax.experimental.pallas import tpu as pltpu
from jax.sharding import Mesh, PartitionSpec as P

NX, NZ, NC, NY, NL = 4, 2, 2, 8, 4
AXES = ("x", "zh", "c", "y", "zl")
REPLICA = ("x", "zh", "c")
FSDP = ("y", "zl")
REPLICAS = NX * NZ * NC
ROWS = 64
OWN = 512
LANES = 128
TILES = OWN // LANES
SUMS = NZ * TILES * ROWS
MOM = TILES * ROWS
REST = 16
MOST = MOM - REST
QUAD = SUMS + MOST + NX * REST
GATHER = SUMS + NZ * MOST
F32, BF16 = jnp.float32, jnp.bfloat16
VMEM = pl.BlockSpec(memory_space=pltpu.VMEM)
HBM = pl.BlockSpec(memory_space=pl.ANY)
SMALL = pltpu.CompilerParams(vmem_limit_bytes=4 * 1024 * 1024)


def near(x):
    return pltpu.with_memory_space_constraint(x, pltpu.VMEM)


def far(x):
    return pltpu.with_memory_space_constraint(x, pltpu.HBM)


def flat(tile):
    return slice(tile * ROWS, (tile + 1) * ROWS)


def block_cols(x, h, core):
    return pl.ds(pl.multiple_of(((x * NZ + h) * NC + core) * OWN, OWN), OWN)


def delta_kernel(own, local_ref, base_ref, *refs):
    out_ref, local_buf, base_buf, sems = refs[-4:]
    core = lax.axis_index("c")
    core = core if own else 1 - core
    copies = []
    for x in range(NX):
        for h in range(NZ):
            cols = block_cols(x, h, core)
            to = slice(h * OWN, (h + 1) * OWN)
            pair = [
                pltpu.make_async_copy(local_ref.at[0, :, cols], local_buf.at[x, :, to], sems.at[0, x, h]),
                pltpu.make_async_copy(base_ref.at[:, cols], base_buf.at[x, :, to], sems.at[1, x, h]),
            ]
            for copy in pair:
                copy.start()
            copies.append((x, h, pair))
    rest = jnp.zeros((REST, LANES), BF16)
    if own:
        rest = refs[0][ROWS - REST:, OWN - LANES:].astype(BF16)
    for x in range(NX):
        out_ref[x, SUMS:, :] = rest
    for x, h, pair in copies:
        for copy in pair:
            copy.wait()
        for t in range(TILES):
            cols = slice(h * OWN + t * LANES, h * OWN + (t + 1) * LANES)
            delta = local_buf[x, :, cols].astype(F32) - base_buf[x, :, cols].astype(F32)
            out_ref[x, flat(h * TILES + t), :] = delta.astype(BF16)


def delta_half(own, local, base, momentum, name):
    buf = pltpu.VMEM((NX, ROWS, NZ * OWN), BF16)
    return pl.pallas_call(
        lambda *refs: delta_kernel(own, *refs),
        in_specs=[HBM, HBM] + [VMEM] * own,
        out_specs=VMEM,
        out_shape=pltpu.VMEM((NX, SUMS + REST, LANES), BF16),
        scratch_shapes=[buf, buf, pltpu.SemaphoreType.DMA((2, NX, NZ))],
        cost_estimate=pl.CostEstimate(flops=2**18, bytes_accessed=3 * 2**19, transcendentals=0),
        compiler_params=SMALL,
        name=name,
    )(far(local), far(base), *([near(momentum)] if own else []))


def quad_kernel(parts_ref, mom_ref, out_ref):
    for t in range(NZ * TILES):
        total = parts_ref[0, flat(t), :].astype(F32)
        for k in range(1, NX):
            total = total + parts_ref[k, flat(t), :].astype(F32)
        out_ref[flat(t), :] = total.astype(BF16)
    for t in range(TILES):
        rows = ROWS - REST if t == TILES - 1 else ROWS
        at = SUMS + t * ROWS
        out_ref[at:at + rows, :] = mom_ref[:rows, t * LANES:(t + 1) * LANES].astype(BF16)
    for k in range(NX):
        at = SUMS + MOST + k * REST
        out_ref[at:at + REST, :] = parts_ref[k, SUMS:, :]


def total_kernel(both_ref, out_ref, squares_ref):
    acc = jnp.zeros((ROWS, LANES), F32)
    for t in range(NZ * TILES):
        total = both_ref[0, flat(t), :].astype(F32) + both_ref[1, flat(t), :].astype(F32)
        total = total.astype(BF16)
        out_ref[flat(t), :] = total
        acc = acc + total.astype(F32) * total.astype(F32)
    for h in range(NZ):
        at = SUMS + h * MOST
        out_ref[at:at + MOST, :] = both_ref[h, SUMS:SUMS + MOST, :]
    squares_ref[...] = jnp.broadcast_to(jnp.sum(acc), squares_ref.shape)


def pack_kernel(shares_ref, both_ref, out_ref):
    for h in range(NZ):
        out_ref[flat(h), :] = both_ref[h, SUMS + MOST:, :].astype(F32)
    out_ref[NZ * ROWS:, :] = jnp.broadcast_to(jnp.sum(shares_ref[:, 0:1]), (8, LANES))


def final_kernel(entries, pack_refs, base_ref, mom_ref, sum_refs, new_ref, newmom_ref, buf, sems):
    core = lax.axis_index("c")
    squares = pack_refs[0][NZ * ROWS:, :] + pack_refs[1][NZ * ROWS:, :]
    mean = jnp.sum(squares[0:1, 0:1]) / (REPLICAS * REPLICAS) / entries
    factor = jnp.minimum(1.0, 0.04 / jnp.sqrt(mean + 1e-06)) / REPLICAS

    def weights(rows, cols, total, mom):
        clipped = factor * total.astype(F32)
        update = 0.7 * (clipped + 0.9 * (0.9 * mom.astype(F32) + clipped))
        buf[rows, cols] = (base_ref[rows, cols].astype(F32) - update).astype(BF16)

    copies = []
    for x in range(NX):
        for which in range(NC):
            sums, pack = sum_refs[which], pack_refs[which]
            owner = core if which == 0 else 1 - core
            for h in range(NZ):
                for t in range(TILES):
                    start = ((x * NZ + h) * NC + owner) * OWN + t * LANES
                    cols = pl.ds(pl.multiple_of(start, LANES), LANES)
                    at = (h * TILES + t) * ROWS
                    mom_at = SUMS + h * MOST + t * ROWS
                    rows = ROWS - REST if t == TILES - 1 else ROWS
                    weights(slice(0, rows), cols, sums[x, at:at + rows, :], sums[x, mom_at:mom_at + rows, :])
                    if rows < ROWS:
                        rest_at = h * ROWS + x * REST
                        weights(slice(rows, ROWS), cols, sums[x, at + rows:at + ROWS, :], pack[rest_at:rest_at + REST, :])
        cols = slice(x * NZ * NC * OWN, (x + 1) * NZ * NC * OWN)
        copies.append(pltpu.make_async_copy(buf.at[:, cols], new_ref.at[:, cols], sems.at[x]))
        copies[-1].start()
    for t in range(TILES):
        at = pl.multiple_of((lax.axis_index("zh") * TILES + t) * ROWS, ROWS)
        total = sum_refs[0][lax.axis_index("x"), pl.ds(at, ROWS), :].astype(F32)
        cols = slice(t * LANES, (t + 1) * LANES)
        newmom_ref[:, cols] = 0.9 * mom_ref[:, cols] + factor * total
    for copy in copies:
        copy.wait()


def per_device(local_weights, global_weights, momentum):
    rows, width = global_weights.shape
    swap = [(0, 1), (1, 0)]
    send = delta_half(False, local_weights, global_weights, momentum, "delta_send")
    keep = delta_half(True, local_weights, global_weights, momentum, "delta_keep")
    pair = (keep.astype(F32) + lax.ppermute(send, "c", swap).astype(F32)).astype(BF16)
    parts = lax.all_to_all(pair, "x", 0, 0, tiled=True)
    quad = pl.pallas_call(
        quad_kernel, in_specs=[VMEM] * 2, out_specs=VMEM, out_shape=pltpu.VMEM((QUAD, LANES), BF16),
        compiler_params=SMALL, name="quad",
    )(near(parts), near(momentum))
    both = lax.all_gather(quad, "zh", axis=0)
    group = NX * NY * NL
    total, squares = pl.pallas_call(
        total_kernel, in_specs=[VMEM], out_specs=[VMEM, VMEM],
        out_shape=[pltpu.VMEM((GATHER, LANES), BF16), pltpu.VMEM((group, 2), F32)],
        compiler_params=SMALL, name="total",
    )(near(both))
    shares = lax.all_to_all(squares, ("x", "y", "zl"), 0, 0, tiled=True)
    own = lax.all_gather(total, "x", axis=0)
    other = lax.ppermute(lax.optimization_barrier((own, shares))[0], "c", swap)
    pack = pl.pallas_call(
        pack_kernel, in_specs=[VMEM] * 2, out_specs=VMEM,
        out_shape=pltpu.VMEM((NZ * ROWS + 8, LANES), F32),
        compiler_params=SMALL, name="pack",
    )(near(shares), near(both))
    other_pack = lax.ppermute(pack, "c", swap)
    entries = rows * width * NY * NL
    return pl.pallas_call(
        lambda p0, p1, base, mom, s0, s1, *refs: final_kernel(entries, (p0, p1), base, mom, (s0, s1), *refs),
        in_specs=[VMEM] * 6, out_specs=[HBM, VMEM],
        out_shape=[jax.ShapeDtypeStruct((rows, width), BF16), jax.ShapeDtypeStruct(momentum.shape, F32)],
        scratch_shapes=[pltpu.VMEM((rows, width), BF16), pltpu.SemaphoreType.DMA((NX,))],
        compiler_params=SMALL, name="final",
    )(near(pack), near(other_pack), near(global_weights), near(momentum), near(own), near(other))


def solution(mesh):
    fine = Mesh(mesh.devices.reshape(NX, NZ, NC, NY, NL), AXES)
    in_specs = (P(REPLICA, FSDP, None), P(FSDP, None), P(FSDP, REPLICA))
    out_specs = (P(FSDP, None), P(FSDP, REPLICA))
    return jax.shard_map(
        per_device, mesh=fine, in_specs=in_specs, out_specs=out_specs, check_vma=False
    )
```

```python
import jax
import jax.numpy as jnp
from jax import lax
from jax.experimental import pallas as pl
from jax.experimental.pallas import tpu as pltpu
from jax.sharding import Mesh, PartitionSpec as P

NX, NZ, NC, NY, NL = 4, 2, 2, 8, 4
AXES = ("x", "zh", "c", "y", "zl")
REPLICA = ("x", "zh", "c")
FSDP = ("y", "zl")
REPLICAS = NX * NZ * NC
ROWS = 64
OWN = 512
LANES = 128
TILES = OWN // LANES
SUMS = NZ * TILES * ROWS
MOM = TILES * ROWS
REST = 16
MOST = MOM - REST
QUAD = SUMS + NX * REST
GATHER = SUMS + NZ * MOST
TILE = 16
RESTS = NX * GATHER
SCALARS = RESTS + NZ * NX * REST
PACK = SCALARS + 3 * TILE
F32, BF16 = jnp.float32, jnp.bfloat16
VMEM = pl.BlockSpec(memory_space=pltpu.VMEM)
HBM = pl.BlockSpec(memory_space=pl.ANY)
SMALL = pltpu.CompilerParams(vmem_limit_bytes=4 * 1024 * 1024)


def near(x):
    return pltpu.with_memory_space_constraint(x, pltpu.VMEM)


def far(x):
    return pltpu.with_memory_space_constraint(x, pltpu.HBM)


def flat(tile):
    return slice(tile * ROWS, (tile + 1) * ROWS)


def block_cols(x, h, core, t):
    return pl.ds(pl.multiple_of(((x * NZ + h) * NC + core) * OWN + t * LANES, LANES), LANES)


def fetch_kernel(local_ref, base_ref, mom_ref, local_out, base_out, rest_out, sems):
    core = lax.axis_index("c")
    copies = [
        pltpu.make_async_copy(
            mom_ref.at[ROWS - REST:, OWN - LANES:], rest_out, sems.at[2 * NX * NZ]
        )
    ]
    for x in range(NX):
        for h in range(NZ):
            start = ((x * NZ + h) * NC + core) * OWN
            cols = pl.ds(pl.multiple_of(start, OWN), OWN)
            to = slice(h * OWN, (h + 1) * OWN)
            at = 2 * (x * NZ + h)
            copies.append(pltpu.make_async_copy(local_ref.at[0, :, cols], local_out.at[x, :, to], sems.at[at]))
            copies.append(pltpu.make_async_copy(base_ref.at[:, cols], base_out.at[x, :, to], sems.at[at + 1]))
    for copy in copies:
        copy.start()
    for copy in copies:
        copy.wait()


def fetch(local, base, momentum):
    half = pltpu.VMEM((NX, ROWS, NZ * OWN), BF16)
    return pl.pallas_call(
        fetch_kernel,
        in_specs=[HBM] * 3,
        out_specs=[VMEM] * 3,
        out_shape=[half, half, pltpu.VMEM((REST, LANES), F32)],
        scratch_shapes=[pltpu.SemaphoreType.DMA((2 * NX * NZ + 1,))],
        cost_estimate=pl.CostEstimate(flops=0, bytes_accessed=2**22, transcendentals=0),
        compiler_params=SMALL,
        name="fetch",
    )(far(local), far(base), far(momentum))


def pair_kernel(local_ref, base_ref, rest_ref, got_ref, out_ref):
    core = lax.axis_index("c")
    for x in range(NX):
        for h in range(NZ):
            for t in range(TILES):
                cols = slice(h * OWN + t * LANES, h * OWN + (t + 1) * LANES)
                base = base_ref[x, :, cols].astype(F32)
                got = got_ref[0, :, block_cols(x, h, core, t)].astype(F32)
                pair = (local_ref[x, :, cols].astype(F32) - base) + (got - base)
                out_ref[x, flat(h * TILES + t), :] = pair.astype(BF16)
        out_ref[x, SUMS:, :] = rest_ref[...].astype(BF16)


def quad_kernel(parts_ref, out_ref):
    for t in range(NZ * TILES):
        total = parts_ref[0, flat(t), :].astype(F32)
        for k in range(1, NX):
            total = total + parts_ref[k, flat(t), :].astype(F32)
        out_ref[flat(t), :] = total.astype(BF16)
    for k in range(NX):
        at = SUMS + k * REST
        out_ref[at:at + REST, :] = parts_ref[k, SUMS:, :]


def total_kernel(both_ref, mine_ref, theirs_ref, out_ref, squares_ref):
    acc = jnp.zeros((ROWS, LANES), F32)
    for t in range(NZ * TILES):
        total = both_ref[0, flat(t), :].astype(F32) + both_ref[1, flat(t), :].astype(F32)
        total = total.astype(BF16)
        out_ref[flat(t), :] = total
        acc = acc + total.astype(F32) * total.astype(F32)
    half = lax.axis_index("zh")
    for t in range(TILES):
        rows = ROWS - REST if t == TILES - 1 else ROWS
        mine = mine_ref[:rows, t * LANES:(t + 1) * LANES]
        theirs = theirs_ref[:rows, t * LANES:(t + 1) * LANES]
        for h in range(NZ):
            at = SUMS + h * MOST + t * ROWS
            out_ref[at:at + rows, :] = jnp.where(half == h, mine, theirs).astype(BF16)
    squares_ref[...] = jnp.broadcast_to(jnp.sum(acc), squares_ref.shape)


def pack_kernel(shares_ref, own_ref, both_ref, out_ref):
    for x in range(NX):
        out_ref[x * GATHER:(x + 1) * GATHER, :] = own_ref[x]
    for h in range(NZ):
        at = RESTS + h * NX * REST
        out_ref[at:at + NX * REST, :] = both_ref[h, SUMS:, :]
    left = jnp.broadcast_to(jnp.sum(shares_ref[:, 0:1]), (TILE, LANES))
    for k in range(3):
        part = left.astype(BF16)
        out_ref[SCALARS + k * TILE:SCALARS + (k + 1) * TILE, :] = part
        left = left - part.astype(F32)


def final_kernel(entries, base_ref, mom_ref, mine_ref, theirs_ref, new_ref, newmom_ref, buf, sems):
    core = lax.axis_index("c")
    squares = 0.0
    for pack in (mine_ref, theirs_ref):
        parts = [jnp.sum(pack[at:at + TILE, :][0:1, 0:1].astype(F32)) for at in range(SCALARS, PACK, TILE)]
        squares = squares + ((parts[2] + parts[1]) + parts[0])
    mean = squares / (REPLICAS * REPLICAS) / entries
    factor = jnp.minimum(1.0, 0.04 / jnp.sqrt(mean + 1e-06)) / REPLICAS
    sum_weight = (0.7 * 1.9) * factor

    def weights(rows, cols, total, mom):
        update = sum_weight * total.astype(F32) + (0.7 * 0.81) * mom.astype(F32)
        buf[rows, cols] = (base_ref[rows, cols].astype(F32) - update).astype(BF16)

    copies = []
    for x in range(NX):
        for which, pack in enumerate((mine_ref, theirs_ref)):
            owner = core if which == 0 else 1 - core
            for h in range(NZ):
                for t in range(TILES):
                    cols = block_cols(x, h, owner, t)
                    at = x * GATHER + (h * TILES + t) * ROWS
                    mom_at = x * GATHER + SUMS + h * MOST + t * ROWS
                    rows = ROWS - REST if t == TILES - 1 else ROWS
                    weights(slice(0, rows), cols, pack[at:at + rows, :], pack[mom_at:mom_at + rows, :])
                    if rows < ROWS:
                        rest_at = RESTS + (h * NX + x) * REST
                        weights(slice(rows, ROWS), cols, pack[at + rows:at + ROWS, :], pack[rest_at:rest_at + REST, :])
        cols = slice(x * NZ * NC * OWN, (x + 1) * NZ * NC * OWN)
        copies.append(pltpu.make_async_copy(buf.at[:, cols], new_ref.at[:, cols], sems.at[x]))
        copies[-1].start()
    for t in range(TILES):
        at = lax.axis_index("x") * GATHER + (lax.axis_index("zh") * TILES + t) * ROWS
        total = mine_ref[pl.ds(pl.multiple_of(at, TILE), ROWS), :].astype(F32)
        cols = slice(t * LANES, (t + 1) * LANES)
        newmom_ref[:, cols] = 0.9 * mom_ref[:, cols] + factor * total
    for copy in copies:
        copy.wait()


def per_device(local_weights, global_weights, momentum):
    rows, width = global_weights.shape
    swap = [(0, 1), (1, 0)]
    theirs = lax.ppermute(momentum, "zh", swap)
    got = lax.ppermute(local_weights, "c", swap)
    mine, base, rest = fetch(local_weights, global_weights, momentum)
    pair = pl.pallas_call(
        pair_kernel, in_specs=[VMEM] * 4, out_specs=VMEM,
        out_shape=pltpu.VMEM((NX, SUMS + REST, LANES), BF16),
        compiler_params=SMALL, name="pair",
    )(near(mine), near(base), near(rest), near(got))
    parts = lax.all_to_all(pair, "x", 0, 0, tiled=True)
    quad = pl.pallas_call(
        quad_kernel, in_specs=[VMEM], out_specs=VMEM, out_shape=pltpu.VMEM((QUAD, LANES), BF16),
        compiler_params=SMALL, name="quad",
    )(near(parts))
    both = lax.all_gather(quad, "zh", axis=0)
    group = NX * NY * NL
    total, squares = pl.pallas_call(
        total_kernel, in_specs=[VMEM] * 3, out_specs=[VMEM, VMEM],
        out_shape=[pltpu.VMEM((GATHER, LANES), BF16), pltpu.VMEM((group, 2), F32)],
        compiler_params=SMALL, name="total",
    )(near(both), near(momentum), near(theirs))
    shares = lax.all_to_all(squares, ("x", "y", "zl"), 0, 0, tiled=True)
    own = lax.all_gather(total, "x", axis=0)
    pack = pl.pallas_call(
        pack_kernel, in_specs=[VMEM] * 3, out_specs=VMEM, out_shape=pltpu.VMEM((PACK, LANES), BF16),
        compiler_params=SMALL, name="pack",
    )(near(shares), near(own), near(both))
    other = lax.ppermute(pack, "c", swap)
    entries = rows * width * NY * NL
    return pl.pallas_call(
        lambda *refs: final_kernel(entries, *refs),
        in_specs=[VMEM] * 4, out_specs=[HBM, VMEM],
        out_shape=[jax.ShapeDtypeStruct((rows, width), BF16), jax.ShapeDtypeStruct(momentum.shape, F32)],
        scratch_shapes=[pltpu.VMEM((rows, width), BF16), pltpu.SemaphoreType.DMA((NX,))],
        compiler_params=SMALL, name="final",
    )(near(global_weights), near(momentum), near(pack), near(other))


def solution(mesh):
    fine = Mesh(mesh.devices.reshape(NX, NZ, NC, NY, NL), AXES)
    in_specs = (P(REPLICA, FSDP, None), P(FSDP, None), P(FSDP, REPLICA))
    out_specs = (P(FSDP, None), P(FSDP, REPLICA))
    return jax.shard_map(
        per_device, mesh=fine, in_specs=in_specs, out_specs=out_specs, check_vma=False
    )
```

```python
import jax
import jax.numpy as jnp
from jax import lax
from jax.experimental import pallas as pl
from jax.experimental.pallas import tpu as pltpu
from jax.sharding import Mesh, PartitionSpec as P

NX, NZ, NC, NY, NL = 4, 2, 2, 8, 4
AXES = ("x", "zh", "c", "y", "zl")
REPLICA = ("x", "zh", "c")
FSDP = ("y", "zl")
REPLICAS = NX * NZ * NC
ROWS = 64
OWN = 512
LANES = 128
TILES = OWN // LANES
SUMS = NZ * TILES * ROWS
MOM = TILES * ROWS
REST = 16
MOST = MOM - REST
QUAD = SUMS + NX * REST
GATHER = SUMS + NZ * MOST
TILE = 16
RESTS = NX * GATHER
SCALARS = RESTS + NZ * NX * REST
PACK = SCALARS + 3 * TILE
F32, BF16 = jnp.float32, jnp.bfloat16
VMEM = pl.BlockSpec(memory_space=pltpu.VMEM)
HBM = pl.BlockSpec(memory_space=pl.ANY)
SMALL = pltpu.CompilerParams(vmem_limit_bytes=4 * 1024 * 1024)


def near(x):
    return pltpu.with_memory_space_constraint(x, pltpu.VMEM)


def far(x):
    return pltpu.with_memory_space_constraint(x, pltpu.HBM)


def flat(tile):
    return slice(tile * ROWS, (tile + 1) * ROWS)


def block_cols(x, h, core, t):
    return pl.ds(pl.multiple_of(((x * NZ + h) * NC + core) * OWN + t * LANES, LANES), LANES)


def fetch_kernel(local_ref, base_ref, mom_ref, local_out, base_out, rest_out, sems):
    core = lax.axis_index("c")
    copies = [
        pltpu.make_async_copy(
            mom_ref.at[ROWS - REST:, OWN - LANES:], rest_out, sems.at[2 * NX * NZ]
        )
    ]
    for x in range(NX):
        for h in range(NZ):
            start = ((x * NZ + h) * NC + core) * OWN
            cols = pl.ds(pl.multiple_of(start, OWN), OWN)
            to = slice(h * OWN, (h + 1) * OWN)
            at = 2 * (x * NZ + h)
            copies.append(pltpu.make_async_copy(local_ref.at[0, :, cols], local_out.at[x, :, to], sems.at[at]))
            copies.append(pltpu.make_async_copy(base_ref.at[:, cols], base_out.at[x, :, to], sems.at[at + 1]))
    for copy in copies:
        copy.start()
    for copy in copies:
        copy.wait()


def fetch(local, base, momentum):
    half = pltpu.VMEM((NX, ROWS, NZ * OWN), BF16)
    return pl.pallas_call(
        fetch_kernel,
        in_specs=[HBM] * 3,
        out_specs=[VMEM] * 3,
        out_shape=[half, half, pltpu.VMEM((REST, LANES), F32)],
        scratch_shapes=[pltpu.SemaphoreType.DMA((2 * NX * NZ + 1,))],
        cost_estimate=pl.CostEstimate(flops=0, bytes_accessed=2**22, transcendentals=0),
        compiler_params=SMALL,
        name="fetch",
    )(far(local), far(base), far(momentum))


def pair_kernel(local_ref, base_ref, rest_ref, got_ref, out_ref):
    core = lax.axis_index("c")
    for x in range(NX):
        for h in range(NZ):
            for t in range(TILES):
                cols = slice(h * OWN + t * LANES, h * OWN + (t + 1) * LANES)
                base = base_ref[x, :, cols].astype(F32)
                got = got_ref[0, :, block_cols(x, h, core, t)].astype(F32)
                pair = (local_ref[x, :, cols].astype(F32) - base) + (got - base)
                out_ref[x, flat(h * TILES + t), :] = pair.astype(BF16)
        out_ref[x, SUMS:, :] = rest_ref[...].astype(BF16)


def quad_kernel(parts_ref, out_ref):
    for t in range(NZ * TILES):
        total = parts_ref[0, flat(t), :].astype(F32)
        for k in range(1, NX):
            total = total + parts_ref[k, flat(t), :].astype(F32)
        out_ref[flat(t), :] = total.astype(BF16)
    for k in range(NX):
        at = SUMS + k * REST
        out_ref[at:at + REST, :] = parts_ref[k, SUMS:, :]


def total_kernel(both_ref, mine_ref, theirs_ref, out_ref, squares_ref):
    acc = jnp.zeros((ROWS, LANES), F32)
    for t in range(NZ * TILES):
        total = both_ref[0, flat(t), :].astype(F32) + both_ref[1, flat(t), :].astype(F32)
        total = total.astype(BF16)
        out_ref[flat(t), :] = total
        acc = acc + total.astype(F32) * total.astype(F32)
    half = lax.axis_index("zh")
    for t in range(TILES):
        rows = ROWS - REST if t == TILES - 1 else ROWS
        mine = mine_ref[:rows, t * LANES:(t + 1) * LANES].astype(BF16)
        theirs = theirs_ref[:rows, t * LANES:(t + 1) * LANES]
        for h in range(NZ):
            at = SUMS + h * MOST + t * ROWS
            out_ref[at:at + rows, :] = jnp.where(half == h, mine, theirs)
    squares_ref[...] = jnp.broadcast_to(jnp.sum(acc), squares_ref.shape)


def pack_kernel(shares_ref, own_ref, both_ref, out_ref):
    for x in range(NX):
        out_ref[x * GATHER:(x + 1) * GATHER, :] = own_ref[x]
    for h in range(NZ):
        at = RESTS + h * NX * REST
        out_ref[at:at + NX * REST, :] = both_ref[h, SUMS:, :]
    left = jnp.broadcast_to(jnp.sum(shares_ref[:, 0:1]), (TILE, LANES))
    for k in range(3):
        part = left.astype(BF16)
        out_ref[SCALARS + k * TILE:SCALARS + (k + 1) * TILE, :] = part
        left = left - part.astype(F32)


def final_kernel(entries, base_ref, mom_ref, mine_ref, theirs_ref, new_ref, newmom_ref, buf, sems):
    core = lax.axis_index("c")
    squares = 0.0
    for pack in (mine_ref, theirs_ref):
        parts = [jnp.sum(pack[at:at + TILE, :][0:1, 0:1].astype(F32)) for at in range(SCALARS, PACK, TILE)]
        squares = squares + ((parts[2] + parts[1]) + parts[0])
    mean = squares / (REPLICAS * REPLICAS) / entries
    factor = jnp.minimum(1.0, 0.04 / jnp.sqrt(mean + 1e-06)) / REPLICAS
    sum_weight = (0.7 * 1.9) * factor

    def weights(rows, cols, total, mom):
        update = sum_weight * total.astype(F32) + (0.7 * 0.81) * mom.astype(F32)
        buf[rows, cols] = (base_ref[rows, cols].astype(F32) - update).astype(BF16)

    copies = []
    for x in range(NX):
        for h in range(NZ):
            for which, pack in enumerate((mine_ref, theirs_ref)):
                owner = core if which == 0 else 1 - core
                for t in range(TILES):
                    cols = block_cols(x, h, owner, t)
                    at = x * GATHER + (h * TILES + t) * ROWS
                    mom_at = x * GATHER + SUMS + h * MOST + t * ROWS
                    rows = ROWS - REST if t == TILES - 1 else ROWS
                    weights(slice(0, rows), cols, pack[at:at + rows, :], pack[mom_at:mom_at + rows, :])
                    if rows < ROWS:
                        rest_at = RESTS + (h * NX + x) * REST
                        weights(slice(rows, ROWS), cols, pack[at + rows:at + ROWS, :], pack[rest_at:rest_at + REST, :])
            at = (x * NZ + h) * NC * OWN
            cols = slice(at, at + NC * OWN)
            copies.append(pltpu.make_async_copy(buf.at[:, cols], new_ref.at[:, cols], sems.at[x * NZ + h]))
            copies[-1].start()
    for t in range(TILES):
        at = lax.axis_index("x") * GATHER + (lax.axis_index("zh") * TILES + t) * ROWS
        total = mine_ref[pl.ds(pl.multiple_of(at, TILE), ROWS), :].astype(F32)
        cols = slice(t * LANES, (t + 1) * LANES)
        newmom_ref[:, cols] = 0.9 * mom_ref[:, cols] + factor * total
    for copy in copies:
        copy.wait()


def per_device(local_weights, global_weights, momentum):
    rows, width = global_weights.shape
    swap = [(0, 1), (1, 0)]
    theirs = lax.ppermute(momentum.astype(BF16), "zh", swap)
    got = lax.ppermute(local_weights, "c", swap)
    mine, base, rest = fetch(local_weights, global_weights, momentum)
    pair = pl.pallas_call(
        pair_kernel, in_specs=[VMEM] * 4, out_specs=VMEM,
        out_shape=pltpu.VMEM((NX, SUMS + REST, LANES), BF16),
        compiler_params=SMALL, name="pair",
    )(near(mine), near(base), near(rest), near(got))
    parts = lax.all_to_all(pair, "x", 0, 0, tiled=True)
    quad = pl.pallas_call(
        quad_kernel, in_specs=[VMEM], out_specs=VMEM, out_shape=pltpu.VMEM((QUAD, LANES), BF16),
        compiler_params=SMALL, name="quad",
    )(near(parts))
    both = lax.all_gather(quad, "zh", axis=0)
    group = NX * NY * NL
    total, squares = pl.pallas_call(
        total_kernel, in_specs=[VMEM] * 3, out_specs=[VMEM, VMEM],
        out_shape=[pltpu.VMEM((GATHER, LANES), BF16), pltpu.VMEM((group, 2), F32)],
        compiler_params=SMALL, name="total",
    )(near(both), near(momentum), near(theirs))
    shares = lax.all_to_all(squares, ("x", "y", "zl"), 0, 0, tiled=True)
    own = lax.all_gather(total, "x", axis=0)
    pack = pl.pallas_call(
        pack_kernel, in_specs=[VMEM] * 3, out_specs=VMEM, out_shape=pltpu.VMEM((PACK, LANES), BF16),
        compiler_params=SMALL, name="pack",
    )(near(shares), near(own), near(both))
    other = lax.ppermute(pack, "c", swap)
    entries = rows * width * NY * NL
    return pl.pallas_call(
        lambda *refs: final_kernel(entries, *refs),
        in_specs=[VMEM] * 4, out_specs=[HBM, VMEM],
        out_shape=[jax.ShapeDtypeStruct((rows, width), BF16), jax.ShapeDtypeStruct(momentum.shape, F32)],
        scratch_shapes=[pltpu.VMEM((rows, width), BF16), pltpu.SemaphoreType.DMA((NX * NZ,))],
        compiler_params=SMALL, name="final",
    )(near(global_weights), near(momentum), near(pack), near(other))


def solution(mesh):
    fine = Mesh(mesh.devices.reshape(NX, NZ, NC, NY, NL), AXES)
    in_specs = (P(REPLICA, FSDP, None), P(FSDP, None), P(FSDP, REPLICA))
    out_specs = (P(FSDP, None), P(FSDP, REPLICA))
    return jax.shard_map(
        per_device, mesh=fine, in_specs=in_specs, out_specs=out_specs, check_vma=False
    )
```

```python
import jax
import jax.numpy as jnp
from jax import lax
from jax.experimental import pallas as pl
from jax.experimental.pallas import tpu as pltpu
from jax.sharding import Mesh, PartitionSpec as P

NX, NZ, NC, NY, NL = 4, 2, 2, 8, 4
AXES = ("x", "zh", "c", "y", "zl")
REPLICA = ("x", "zh", "c")
FSDP = ("y", "zl")
REPLICAS = NX * NZ * NC
ROWS = 64
OWN = 512
LANES = 128
TILES = OWN // LANES
SUMS = NZ * TILES * ROWS
MOM = TILES * ROWS
REST = 16
MOST = MOM - REST
QUAD = SUMS + NX * REST
GATHER = SUMS + NZ * MOST
TILE = 16
RESTS = NX * GATHER
SCALARS = RESTS + NZ * NX * REST
PACK = SCALARS + 3 * TILE
F32, BF16 = jnp.float32, jnp.bfloat16
VMEM = pl.BlockSpec(memory_space=pltpu.VMEM)
HBM = pl.BlockSpec(memory_space=pl.ANY)
SMALL = pltpu.CompilerParams(vmem_limit_bytes=4 * 1024 * 1024)


def near(x):
    return pltpu.with_memory_space_constraint(x, pltpu.VMEM)


def far(x):
    return pltpu.with_memory_space_constraint(x, pltpu.HBM)


def flat(tile):
    return slice(tile * ROWS, (tile + 1) * ROWS)


def block_cols(x, h, core, t):
    return pl.ds(pl.multiple_of(((x * NZ + h) * NC + core) * OWN + t * LANES, LANES), LANES)


def fetch_kernel(local_ref, base_ref, mom_ref, local_out, base_out, rest_out, sems):
    core = lax.axis_index("c")
    copies = [
        pltpu.make_async_copy(
            mom_ref.at[ROWS - REST:, OWN - LANES:], rest_out, sems.at[2 * NX * NZ]
        )
    ]
    for x in range(NX):
        for h in range(NZ):
            start = ((x * NZ + h) * NC + core) * OWN
            cols = pl.ds(pl.multiple_of(start, OWN), OWN)
            to = slice(h * OWN, (h + 1) * OWN)
            at = 2 * (x * NZ + h)
            copies.append(pltpu.make_async_copy(local_ref.at[0, :, cols], local_out.at[x, :, to], sems.at[at]))
            copies.append(pltpu.make_async_copy(base_ref.at[:, cols], base_out.at[x, :, to], sems.at[at + 1]))
    for copy in copies:
        copy.start()
    for copy in copies:
        copy.wait()


def fetch(local, base, momentum):
    half = pltpu.VMEM((NX, ROWS, NZ * OWN), BF16)
    return pl.pallas_call(
        fetch_kernel,
        in_specs=[HBM] * 3,
        out_specs=[VMEM] * 3,
        out_shape=[half, half, pltpu.VMEM((REST, LANES), F32)],
        scratch_shapes=[pltpu.SemaphoreType.DMA((2 * NX * NZ + 1,))],
        cost_estimate=pl.CostEstimate(flops=0, bytes_accessed=2**22, transcendentals=0),
        compiler_params=SMALL,
        name="fetch",
    )(far(local), far(base), far(momentum))


def pair_kernel(local_ref, base_ref, rest_ref, got_ref, out_ref, buf, sems):
    core = lax.axis_index("c")
    copies = []
    for x in range(NX):
        for h in range(NZ):
            for t in range(TILES):
                cols = slice(h * OWN + t * LANES, h * OWN + (t + 1) * LANES)
                base = base_ref[x, :, cols].astype(F32)
                got = got_ref[0, :, block_cols(x, h, core, t)].astype(F32)
                pair = (local_ref[x, :, cols].astype(F32) - base) + (got - base)
                buf[x, flat(h * TILES + t), :] = pair.astype(BF16)
        buf[x, SUMS:, :] = rest_ref[...].astype(BF16)
        copies.append(pltpu.make_async_copy(buf.at[x], out_ref.at[x], sems.at[x]))
        copies[-1].start()
    for copy in copies:
        copy.wait()


def quad_kernel(parts_ref, out_ref):
    for t in range(NZ * TILES):
        total = parts_ref[0, flat(t), :].astype(F32)
        for k in range(1, NX):
            total = total + parts_ref[k, flat(t), :].astype(F32)
        out_ref[flat(t), :] = total.astype(BF16)
    for k in range(NX):
        at = SUMS + k * REST
        out_ref[at:at + REST, :] = parts_ref[k, SUMS:, :]


def total_kernel(both_ref, mine_ref, theirs_ref, out_ref, squares_ref, buf, sem):
    acc = jnp.zeros((ROWS, LANES), F32)
    for t in range(NZ * TILES):
        total = both_ref[0, flat(t), :].astype(F32) + both_ref[1, flat(t), :].astype(F32)
        total = total.astype(BF16)
        out_ref[flat(t), :] = total
        acc = acc + total.astype(F32) * total.astype(F32)
    buf[...] = jnp.broadcast_to(jnp.sum(acc), buf.shape)
    copy = pltpu.make_async_copy(buf, squares_ref, sem)
    copy.start()
    half = lax.axis_index("zh")
    for t in range(TILES):
        rows = ROWS - REST if t == TILES - 1 else ROWS
        mine = mine_ref[:rows, t * LANES:(t + 1) * LANES].astype(BF16)
        theirs = theirs_ref[:rows, t * LANES:(t + 1) * LANES]
        for h in range(NZ):
            at = SUMS + h * MOST + t * ROWS
            out_ref[at:at + rows, :] = jnp.where(half == h, mine, theirs)
    copy.wait()


def pack_kernel(shares_ref, own_ref, both_ref, out_ref):
    for x in range(NX):
        out_ref[x * GATHER:(x + 1) * GATHER, :] = own_ref[x]
    for h in range(NZ):
        at = RESTS + h * NX * REST
        out_ref[at:at + NX * REST, :] = both_ref[h, SUMS:, :]
    left = jnp.broadcast_to(jnp.sum(shares_ref[:, 0:1]), (TILE, LANES))
    for k in range(3):
        part = left.astype(BF16)
        out_ref[SCALARS + k * TILE:SCALARS + (k + 1) * TILE, :] = part
        left = left - part.astype(F32)


def final_kernel(entries, base_ref, mom_ref, mine_ref, theirs_ref, new_ref, newmom_ref, buf, sems):
    core = lax.axis_index("c")
    squares = jnp.zeros((8, LANES), F32)
    for pack in (mine_ref, theirs_ref):
        parts = [pack[at:at + TILE, :].astype(F32)[:8] for at in range(SCALARS, PACK, TILE)]
        squares = squares + ((parts[2] + parts[1]) + parts[0])
    mean = squares / (REPLICAS * REPLICAS) / entries
    factor = jnp.minimum(1.0, 0.04 / jnp.sqrt(mean + 1e-06)) / REPLICAS
    sum_weight = (0.7 * 1.9) * factor

    def weights(rows, cols, total, mom):
        scaled = (total.astype(F32).reshape(-1, 8, LANES) * sum_weight[None]).reshape(-1, LANES)
        update = scaled + (0.7 * 0.81) * mom.astype(F32)
        buf[rows, cols] = (base_ref[rows, cols].astype(F32) - update).astype(BF16)

    copies = []
    for x in range(NX):
        for h in range(NZ):
            for which, pack in enumerate((mine_ref, theirs_ref)):
                owner = core if which == 0 else 1 - core
                for t in range(TILES):
                    cols = block_cols(x, h, owner, t)
                    at = x * GATHER + (h * TILES + t) * ROWS
                    mom_at = x * GATHER + SUMS + h * MOST + t * ROWS
                    rows = ROWS - REST if t == TILES - 1 else ROWS
                    weights(slice(0, rows), cols, pack[at:at + rows, :], pack[mom_at:mom_at + rows, :])
                    if rows < ROWS:
                        rest_at = RESTS + (h * NX + x) * REST
                        weights(slice(rows, ROWS), cols, pack[at + rows:at + ROWS, :], pack[rest_at:rest_at + REST, :])
            at = (x * NZ + h) * NC * OWN
            cols = slice(at, at + NC * OWN)
            copies.append(pltpu.make_async_copy(buf.at[:, cols], new_ref.at[:, cols], sems.at[x * NZ + h]))
            copies[-1].start()
    for t in range(TILES):
        at = lax.axis_index("x") * GATHER + (lax.axis_index("zh") * TILES + t) * ROWS
        total = mine_ref[pl.ds(pl.multiple_of(at, TILE), ROWS), :].astype(F32)
        cols = slice(t * LANES, (t + 1) * LANES)
        scaled = (total.reshape(-1, 8, LANES) * factor[None]).reshape(-1, LANES)
        newmom_ref[:, cols] = 0.9 * mom_ref[:, cols] + scaled
    for copy in copies:
        copy.wait()


def per_device(local_weights, global_weights, momentum):
    rows, width = global_weights.shape
    swap = [(0, 1), (1, 0)]
    theirs = lax.ppermute(momentum.astype(BF16), "zh", swap)
    got = lax.ppermute(local_weights, "c", swap)
    mine, base, rest = fetch(local_weights, global_weights, momentum)
    pair = pl.pallas_call(
        pair_kernel, in_specs=[VMEM] * 4, out_specs=HBM,
        out_shape=jax.ShapeDtypeStruct((NX, SUMS + REST, LANES), BF16),
        scratch_shapes=[pltpu.VMEM((NX, SUMS + REST, LANES), BF16), pltpu.SemaphoreType.DMA((NX,))],
        compiler_params=SMALL, name="pair",
    )(near(mine), near(base), near(rest), near(got))
    parts = lax.all_to_all(pair, "x", 0, 0, tiled=True)
    quad = pl.pallas_call(
        quad_kernel, in_specs=[VMEM], out_specs=VMEM, out_shape=pltpu.VMEM((QUAD, LANES), BF16),
        compiler_params=SMALL, name="quad",
    )(near(parts))
    both = lax.all_gather(quad, "zh", axis=0)
    group = NX * NY * NL
    total, squares = pl.pallas_call(
        total_kernel, in_specs=[VMEM] * 3, out_specs=[VMEM, HBM],
        out_shape=[pltpu.VMEM((GATHER, LANES), BF16), jax.ShapeDtypeStruct((group, 2), F32)],
        scratch_shapes=[pltpu.VMEM((group, 2), F32), pltpu.SemaphoreType.DMA],
        compiler_params=SMALL, name="total",
    )(near(both), near(momentum), near(theirs))
    shares = lax.all_to_all(squares, ("x", "y", "zl"), 0, 0, tiled=True)
    own = lax.all_gather(total, "x", axis=0)
    pack = pl.pallas_call(
        pack_kernel, in_specs=[VMEM] * 3, out_specs=VMEM, out_shape=pltpu.VMEM((PACK, LANES), BF16),
        compiler_params=SMALL, name="pack",
    )(near(shares), near(own), near(both))
    other = lax.ppermute(pack, "c", swap)
    entries = rows * width * NY * NL
    return pl.pallas_call(
        lambda *refs: final_kernel(entries, *refs),
        in_specs=[VMEM] * 4, out_specs=[HBM, VMEM],
        out_shape=[jax.ShapeDtypeStruct((rows, width), BF16), jax.ShapeDtypeStruct(momentum.shape, F32)],
        scratch_shapes=[pltpu.VMEM((rows, width), BF16), pltpu.SemaphoreType.DMA((NX * NZ,))],
        compiler_params=SMALL, name="final",
    )(near(global_weights), near(momentum), near(pack), near(other))


def solution(mesh):
    fine = Mesh(mesh.devices.reshape(NX, NZ, NC, NY, NL), AXES)
    in_specs = (P(REPLICA, FSDP, None), P(FSDP, None), P(FSDP, REPLICA))
    out_specs = (P(FSDP, None), P(FSDP, REPLICA))
    return jax.shard_map(
        per_device, mesh=fine, in_specs=in_specs, out_specs=out_specs, check_vma=False
    )
```

```python
import jax
import jax.numpy as jnp
from jax import lax
from jax.experimental import pallas as pl
from jax.experimental.pallas import tpu as pltpu
from jax.sharding import Mesh, PartitionSpec as P

NX, NZ, NC, NY, NL = 4, 2, 2, 8, 4
AXES = ("x", "zh", "c", "y", "zl")
REPLICA = ("x", "zh", "c")
FSDP = ("y", "zl")
REPLICAS = NX * NZ * NC
ROWS = 64
OWN = 512
LANES = 128
TILES = OWN // LANES
SUMS = NZ * TILES * ROWS
MOM = TILES * ROWS
TILE = 16
HALF = TILE // 2
MAIN = MOM - TILE
QUAD = SUMS + NX * HALF
LAST = SUMS + NZ * MAIN
GATHER = LAST + TILE
RESTS = NX * GATHER
SCALARS = RESTS + NZ * NX * HALF
PACK = SCALARS + 3 * TILE
F32, BF16 = jnp.float32, jnp.bfloat16
VMEM = pl.BlockSpec(memory_space=pltpu.VMEM)
HBM = pl.BlockSpec(memory_space=pl.ANY)
SMALL = pltpu.CompilerParams(vmem_limit_bytes=4 * 1024 * 1024)


def near(x):
    return pltpu.with_memory_space_constraint(x, pltpu.VMEM)


def far(x):
    return pltpu.with_memory_space_constraint(x, pltpu.HBM)


def flat(tile):
    return slice(tile * ROWS, (tile + 1) * ROWS)


def block_cols(x, h, core, t):
    return pl.ds(pl.multiple_of(((x * NZ + h) * NC + core) * OWN + t * LANES, LANES), LANES)


def fetch_kernel(local_ref, base_ref, mom_ref, local_out, base_out, rest_out, sems):
    core = lax.axis_index("c")
    copies = [
        pltpu.make_async_copy(
            mom_ref.at[ROWS - TILE:, OWN - LANES:], rest_out, sems.at[2 * NX * NZ]
        )
    ]
    for x in range(NX):
        for h in range(NZ):
            start = ((x * NZ + h) * NC + core) * OWN
            cols = pl.ds(pl.multiple_of(start, OWN), OWN)
            to = slice(h * OWN, (h + 1) * OWN)
            at = 2 * (x * NZ + h)
            copies.append(pltpu.make_async_copy(local_ref.at[0, :, cols], local_out.at[x, :, to], sems.at[at]))
            copies.append(pltpu.make_async_copy(base_ref.at[:, cols], base_out.at[x, :, to], sems.at[at + 1]))
    for copy in copies:
        copy.start()
    for copy in copies:
        copy.wait()


def fetch(local, base, momentum):
    half = pltpu.VMEM((NX, ROWS, NZ * OWN), BF16)
    return pl.pallas_call(
        fetch_kernel,
        in_specs=[HBM] * 3,
        out_specs=[VMEM] * 3,
        out_shape=[half, half, pltpu.VMEM((TILE, LANES), F32)],
        scratch_shapes=[pltpu.SemaphoreType.DMA((2 * NX * NZ + 1,))],
        cost_estimate=pl.CostEstimate(flops=0, bytes_accessed=2**22, transcendentals=0),
        compiler_params=SMALL,
        name="fetch",
    )(far(local), far(base), far(momentum))


def pair_kernel(local_ref, base_ref, rest_ref, got_ref, out_ref, buf, sems):
    core = lax.axis_index("c")
    copies = []
    for x in range(NX):
        for h in range(NZ):
            for t in range(TILES):
                cols = slice(h * OWN + t * LANES, h * OWN + (t + 1) * LANES)
                base = base_ref[x, :, cols].astype(F32)
                got = got_ref[0, :, block_cols(x, h, core, t)].astype(F32)
                pair = (local_ref[x, :, cols].astype(F32) - base) + (got - base)
                buf[x, flat(h * TILES + t), :] = pair.astype(BF16)
        buf[x, SUMS:, :] = rest_ref[...].astype(BF16)
        copies.append(pltpu.make_async_copy(buf.at[x], out_ref.at[x], sems.at[x]))
        copies[-1].start()
    for copy in copies:
        copy.wait()


def quad_kernel(parts_ref, out_ref):
    for t in range(NZ * TILES):
        total = parts_ref[0, flat(t), :].astype(F32)
        for k in range(1, NX):
            total = total + parts_ref[k, flat(t), :].astype(F32)
        out_ref[flat(t), :] = total.astype(BF16)
    for k in range(0, NX, 2):
        last = [parts_ref[k + i, SUMS:, :].astype(F32)[HALF:] for i in range(2)]
        at = SUMS + k * HALF
        out_ref[at:at + TILE, :] = jnp.concatenate(last, axis=0).astype(BF16)


def total_kernel(both_ref, mine_ref, theirs_ref, out_ref, squares_ref, buf, sem):
    acc = jnp.zeros((ROWS, LANES), F32)
    for t in range(NZ * TILES):
        total = both_ref[0, flat(t), :].astype(F32) + both_ref[1, flat(t), :].astype(F32)
        total = total.astype(BF16)
        out_ref[flat(t), :] = total
        acc = acc + total.astype(F32) * total.astype(F32)
    buf[...] = jnp.broadcast_to(jnp.sum(acc), buf.shape)
    copy = pltpu.make_async_copy(buf, squares_ref, sem)
    copy.start()
    half = lax.axis_index("zh")
    last = []
    for t in range(TILES):
        rows = ROWS - TILE if t == TILES - 1 else ROWS
        cols = slice(t * LANES, (t + 1) * LANES)
        mine, theirs = mine_ref[:, cols], theirs_ref[:, cols].astype(F32)
        for h in range(NZ):
            mom = jnp.where(half == h, mine, theirs)
            at = SUMS + h * MAIN + t * ROWS
            out_ref[at:at + rows, :] = mom[:rows].astype(BF16)
            if rows < ROWS:
                last.append(mom[rows:rows + HALF])
    out_ref[LAST:, :] = jnp.concatenate(last, axis=0).astype(BF16)
    copy.wait()


def pack_kernel(shares_ref, own_ref, both_ref, out_ref):
    for x in range(NX):
        out_ref[x * GATHER:(x + 1) * GATHER, :] = own_ref[x]
    for h in range(NZ):
        at = RESTS + h * NX * HALF
        out_ref[at:at + NX * HALF, :] = both_ref[h, SUMS:, :]
    left = jnp.broadcast_to(jnp.sum(shares_ref[:, 0:1]), (TILE, LANES))
    for k in range(3):
        part = left.astype(BF16)
        out_ref[SCALARS + k * TILE:SCALARS + (k + 1) * TILE, :] = part
        left = left - part.astype(F32)


def final_kernel(entries, base_ref, mom_ref, mine_ref, theirs_ref, new_ref, newmom_ref, buf, sems):
    core = lax.axis_index("c")
    squares = jnp.zeros((8, LANES), F32)
    for pack in (mine_ref, theirs_ref):
        parts = [pack[at:at + TILE, :].astype(F32)[:8] for at in range(SCALARS, PACK, TILE)]
        squares = squares + ((parts[2] + parts[1]) + parts[0])
    mean = squares / (REPLICAS * REPLICAS) / entries
    factor = jnp.minimum(1.0, 0.04 / jnp.sqrt(mean + 1e-06)) / REPLICAS
    sum_weight = (0.7 * 1.9) * factor

    def weights(rows, cols, total, mom):
        scaled = (total.astype(F32).reshape(-1, 8, LANES) * sum_weight[None]).reshape(-1, LANES)
        update = scaled + (0.7 * 0.81) * mom
        buf[rows, cols] = (base_ref[rows, cols].astype(F32) - update).astype(BF16)

    copies = []
    for x in range(NX):
        for h in range(NZ):
            for which, pack in enumerate((mine_ref, theirs_ref)):
                owner = core if which == 0 else 1 - core
                for t in range(TILES):
                    cols = block_cols(x, h, owner, t)
                    at = x * GATHER + (h * TILES + t) * ROWS
                    mom_at = x * GATHER + SUMS + h * MAIN + t * ROWS
                    rows = ROWS - TILE if t == TILES - 1 else ROWS
                    mom = pack[mom_at:mom_at + rows, :].astype(F32)
                    weights(slice(0, rows), cols, pack[at:at + rows, :], mom)
                    if rows < ROWS:
                        last_at = x * GATHER + LAST
                        rest_at = RESTS + (h * NX + x) // 2 * TILE
                        last = pack[last_at:last_at + TILE, :].astype(F32)[h * HALF:(h + 1) * HALF]
                        rest = pack[rest_at:rest_at + TILE, :].astype(F32)[x % 2 * HALF:(x % 2 + 1) * HALF]
                        mom = jnp.concatenate([last, rest], axis=0)
                        weights(slice(rows, ROWS), cols, pack[at + rows:at + ROWS, :], mom)
            at = (x * NZ + h) * NC * OWN
            cols = slice(at, at + NC * OWN)
            copies.append(pltpu.make_async_copy(buf.at[:, cols], new_ref.at[:, cols], sems.at[x * NZ + h]))
            copies[-1].start()
    for t in range(TILES):
        at = lax.axis_index("x") * GATHER + (lax.axis_index("zh") * TILES + t) * ROWS
        total = mine_ref[pl.ds(pl.multiple_of(at, TILE), ROWS), :].astype(F32)
        cols = slice(t * LANES, (t + 1) * LANES)
        scaled = (total.reshape(-1, 8, LANES) * factor[None]).reshape(-1, LANES)
        newmom_ref[:, cols] = 0.9 * mom_ref[:, cols] + scaled
    for copy in copies:
        copy.wait()


def per_device(local_weights, global_weights, momentum):
    rows, width = global_weights.shape
    swap = [(0, 1), (1, 0)]
    theirs = lax.ppermute(momentum.astype(BF16), "zh", swap)
    got = lax.ppermute(local_weights, "c", swap)
    mine, base, rest = fetch(local_weights, global_weights, momentum)
    pair = pl.pallas_call(
        pair_kernel, in_specs=[VMEM] * 4, out_specs=HBM,
        out_shape=jax.ShapeDtypeStruct((NX, SUMS + TILE, LANES), BF16),
        scratch_shapes=[pltpu.VMEM((NX, SUMS + TILE, LANES), BF16), pltpu.SemaphoreType.DMA((NX,))],
        compiler_params=SMALL, name="pair",
    )(near(mine), near(base), near(rest), near(got))
    parts = lax.all_to_all(pair, "x", 0, 0, tiled=True)
    quad = pl.pallas_call(
        quad_kernel, in_specs=[VMEM], out_specs=VMEM, out_shape=pltpu.VMEM((QUAD, LANES), BF16),
        compiler_params=SMALL, name="quad",
    )(near(parts))
    both = lax.all_gather(quad, "zh", axis=0)
    group = NX * NY * NL
    total, squares = pl.pallas_call(
        total_kernel, in_specs=[VMEM] * 3, out_specs=[VMEM, HBM],
        out_shape=[pltpu.VMEM((GATHER, LANES), BF16), jax.ShapeDtypeStruct((group, 128), F32)],
        scratch_shapes=[pltpu.VMEM((group, 128), F32), pltpu.SemaphoreType.DMA],
        compiler_params=SMALL, name="total",
    )(near(both), near(momentum), near(theirs))
    shares = lax.all_to_all(squares, ("x", "y", "zl"), 0, 0, tiled=True)
    own = lax.all_gather(total, "x", axis=0)
    pack = pl.pallas_call(
        pack_kernel, in_specs=[VMEM] * 3, out_specs=VMEM, out_shape=pltpu.VMEM((PACK, LANES), BF16),
        compiler_params=SMALL, name="pack",
    )(near(shares), near(own), near(both))
    other = lax.ppermute(pack, "c", swap)
    entries = rows * width * NY * NL
    return pl.pallas_call(
        lambda *refs: final_kernel(entries, *refs),
        in_specs=[VMEM] * 4, out_specs=[HBM, VMEM],
        out_shape=[jax.ShapeDtypeStruct((rows, width), BF16), jax.ShapeDtypeStruct(momentum.shape, F32)],
        scratch_shapes=[pltpu.VMEM((rows, width), BF16), pltpu.SemaphoreType.DMA((NX * NZ,))],
        compiler_params=SMALL, name="final",
    )(near(global_weights), near(momentum), near(pack), near(other))


def solution(mesh):
    fine = Mesh(mesh.devices.reshape(NX, NZ, NC, NY, NL), AXES)
    in_specs = (P(REPLICA, FSDP, None), P(FSDP, None), P(FSDP, REPLICA))
    out_specs = (P(FSDP, None), P(FSDP, REPLICA))
    return jax.shard_map(
        per_device, mesh=fine, in_specs=in_specs, out_specs=out_specs, check_vma=False
    )
```

```python
import jax
import jax.numpy as jnp
from jax import lax
from jax.experimental import pallas as pl
from jax.experimental.pallas import tpu as pltpu
from jax.sharding import Mesh, PartitionSpec as P

NX, NZ, NC, NY, NL = 4, 2, 2, 8, 4
AXES = ("x", "zh", "c", "y", "zl")
REPLICA = ("x", "zh", "c")
FSDP = ("y", "zl")
REPLICAS = NX * NZ * NC
ROWS = 64
OWN = 512
LANES = 128
TILES = OWN // LANES
SUMS = NZ * TILES * ROWS
MOM = TILES * ROWS
TILE = 16
HALF = TILE // 2
MAIN = MOM - TILE
QUAD = SUMS + NX * HALF
LAST = SUMS + NZ * MAIN
GATHER = LAST + TILE
RESTS = NX * GATHER
SCALARS = RESTS + NZ * NX * HALF
PACK = SCALARS + 3 * TILE
F32, BF16 = jnp.float32, jnp.bfloat16
VMEM = pl.BlockSpec(memory_space=pltpu.VMEM)
HBM = pl.BlockSpec(memory_space=pl.ANY)
SMALL = pltpu.CompilerParams(vmem_limit_bytes=4 * 1024 * 1024)


def near(x):
    return pltpu.with_memory_space_constraint(x, pltpu.VMEM)


def far(x):
    return pltpu.with_memory_space_constraint(x, pltpu.HBM)


def flat(tile):
    return slice(tile * ROWS, (tile + 1) * ROWS)


def block_cols(x, h, core, t):
    return pl.ds(pl.multiple_of(((x * NZ + h) * NC + core) * OWN + t * LANES, LANES), LANES)


def fetch_kernel(local_ref, base_ref, mom_ref, local_out, base_out, rest_out, sems):
    core = lax.axis_index("c")
    copies = [
        pltpu.make_async_copy(
            mom_ref.at[ROWS - TILE:, OWN - LANES:], rest_out, sems.at[2 * NX * NZ]
        )
    ]
    for x in range(NX):
        for h in range(NZ):
            start = ((x * NZ + h) * NC + core) * OWN
            cols = pl.ds(pl.multiple_of(start, OWN), OWN)
            to = slice(h * OWN, (h + 1) * OWN)
            at = 2 * (x * NZ + h)
            copies.append(pltpu.make_async_copy(local_ref.at[0, :, cols], local_out.at[x, :, to], sems.at[at]))
            copies.append(pltpu.make_async_copy(base_ref.at[:, cols], base_out.at[x, :, to], sems.at[at + 1]))
    for copy in copies:
        copy.start()
    for copy in copies:
        copy.wait()


def fetch(local, base, momentum):
    half = pltpu.VMEM((NX, ROWS, NZ * OWN), BF16)
    return pl.pallas_call(
        fetch_kernel,
        in_specs=[HBM] * 3,
        out_specs=[VMEM] * 3,
        out_shape=[half, half, pltpu.VMEM((TILE, LANES), F32)],
        scratch_shapes=[pltpu.SemaphoreType.DMA((2 * NX * NZ + 1,))],
        cost_estimate=pl.CostEstimate(flops=0, bytes_accessed=2**22, transcendentals=0),
        compiler_params=SMALL,
        name="fetch",
    )(far(local), far(base), far(momentum))


def pair_kernel(local_ref, base_ref, rest_ref, got_ref, out_ref, buf, sems):
    core = lax.axis_index("c")
    copies = []
    for x in range(NX):
        for h in range(NZ):
            for t in range(TILES):
                cols = slice(h * OWN + t * LANES, h * OWN + (t + 1) * LANES)
                base = base_ref[x, :, cols].astype(F32)
                got = got_ref[0, :, block_cols(x, h, core, t)].astype(F32)
                pair = (local_ref[x, :, cols].astype(F32) - base) + (got - base)
                buf[x, flat(h * TILES + t), :] = pair.astype(BF16)
        buf[x, SUMS:, :] = rest_ref[...].astype(BF16)
        copies.append(pltpu.make_async_copy(buf.at[x], out_ref.at[x], sems.at[x]))
        copies[-1].start()
    for copy in copies:
        copy.wait()


def quad_kernel(parts_ref, out_ref):
    for t in range(NZ * TILES):
        total = parts_ref[0, flat(t), :].astype(F32)
        for k in range(1, NX):
            total = total + parts_ref[k, flat(t), :].astype(F32)
        out_ref[flat(t), :] = total.astype(BF16)
    for k in range(0, NX, 2):
        last = [parts_ref[k + i, SUMS:, :].astype(F32)[HALF:] for i in range(2)]
        at = SUMS + k * HALF
        out_ref[at:at + TILE, :] = jnp.concatenate(last, axis=0).astype(BF16)


def total_kernel(both_ref, mine_ref, theirs_ref, out_ref, squares_ref, buf, sem):
    acc = jnp.zeros((ROWS, LANES), F32)
    for t in range(NZ * TILES):
        total = both_ref[0, flat(t), :].astype(F32) + both_ref[1, flat(t), :].astype(F32)
        total = total.astype(BF16)
        out_ref[flat(t), :] = total
        acc = acc + total.astype(F32) * total.astype(F32)
    buf[...] = jnp.broadcast_to(jnp.sum(acc), buf.shape)
    copy = pltpu.make_async_copy(buf, squares_ref, sem)
    copy.start()
    half = lax.axis_index("zh")
    last = []
    for t in range(TILES):
        rows = ROWS - TILE if t == TILES - 1 else ROWS
        cols = slice(t * LANES, (t + 1) * LANES)
        mine, theirs = mine_ref[:, cols], theirs_ref[:, cols].astype(F32)
        for h in range(NZ):
            mom = jnp.where(half == h, mine, theirs)
            at = SUMS + h * MAIN + t * ROWS
            out_ref[at:at + rows, :] = mom[:rows].astype(BF16)
            if rows < ROWS:
                last.append(mom[rows:rows + HALF])
    out_ref[LAST:, :] = jnp.concatenate(last, axis=0).astype(BF16)
    copy.wait()


def pack_kernel(shares_ref, own_ref, both_ref, out_ref):
    for x in range(NX):
        out_ref[x * GATHER:(x + 1) * GATHER, :] = own_ref[x]
    for h in range(NZ):
        at = RESTS + h * NX * HALF
        out_ref[at:at + NX * HALF, :] = both_ref[h, SUMS:, :]
    left = jnp.broadcast_to(jnp.sum(shares_ref[:, 0:1]), (TILE, LANES))
    for k in range(3):
        part = left.astype(BF16)
        out_ref[SCALARS + k * TILE:SCALARS + (k + 1) * TILE, :] = part
        left = left - part.astype(F32)


def final_kernel(entries, base_ref, mom_ref, mine_ref, theirs_ref, new_ref, newmom_ref, buf, mom_buf, sems, mom_sem):
    core = lax.axis_index("c")
    squares = jnp.zeros((8, LANES), F32)
    for pack in (mine_ref, theirs_ref):
        parts = [pack[at:at + TILE, :].astype(F32)[:8] for at in range(SCALARS, PACK, TILE)]
        squares = squares + ((parts[2] + parts[1]) + parts[0])
    mean = squares / (REPLICAS * REPLICAS) / entries
    factor = jnp.minimum(1.0, 0.04 / jnp.sqrt(mean + 1e-06)) / REPLICAS
    sum_weight = (0.7 * 1.9) * factor

    def weights(rows, cols, total, mom):
        scaled = (total.astype(F32).reshape(-1, 8, LANES) * sum_weight[None]).reshape(-1, LANES)
        update = scaled + (0.7 * 0.81) * mom
        buf[rows, cols] = (base_ref[rows, cols].astype(F32) - update).astype(BF16)

    for t in range(TILES):
        at = lax.axis_index("x") * GATHER + (lax.axis_index("zh") * TILES + t) * ROWS
        total = mine_ref[pl.ds(pl.multiple_of(at, TILE), ROWS), :].astype(F32)
        cols = slice(t * LANES, (t + 1) * LANES)
        scaled = (total.reshape(-1, 8, LANES) * factor[None]).reshape(-1, LANES)
        mom_buf[:, cols] = 0.9 * mom_ref[:, cols] + scaled
    copies = [pltpu.make_async_copy(mom_buf, newmom_ref, mom_sem)]
    copies[0].start()
    for x in range(NX):
        for h in range(NZ):
            for which, pack in enumerate((mine_ref, theirs_ref)):
                owner = core if which == 0 else 1 - core
                for t in range(TILES):
                    cols = block_cols(x, h, owner, t)
                    at = x * GATHER + (h * TILES + t) * ROWS
                    mom_at = x * GATHER + SUMS + h * MAIN + t * ROWS
                    rows = ROWS - TILE if t == TILES - 1 else ROWS
                    mom = pack[mom_at:mom_at + rows, :].astype(F32)
                    weights(slice(0, rows), cols, pack[at:at + rows, :], mom)
                    if rows < ROWS:
                        last_at = x * GATHER + LAST
                        rest_at = RESTS + (h * NX + x) // 2 * TILE
                        last = pack[last_at:last_at + TILE, :].astype(F32)[h * HALF:(h + 1) * HALF]
                        rest = pack[rest_at:rest_at + TILE, :].astype(F32)[x % 2 * HALF:(x % 2 + 1) * HALF]
                        mom = jnp.concatenate([last, rest], axis=0)
                        weights(slice(rows, ROWS), cols, pack[at + rows:at + ROWS, :], mom)
            at = (x * NZ + h) * NC * OWN
            cols = slice(at, at + NC * OWN)
            copies.append(pltpu.make_async_copy(buf.at[:, cols], new_ref.at[:, cols], sems.at[x * NZ + h]))
            copies[-1].start()
    for copy in copies:
        copy.wait()


def per_device(local_weights, global_weights, momentum):
    rows, width = global_weights.shape
    swap = [(0, 1), (1, 0)]
    theirs = lax.ppermute(momentum.astype(BF16), "zh", swap)
    got = lax.ppermute(local_weights, "c", swap)
    mine, base, rest = fetch(local_weights, global_weights, momentum)
    pair = pl.pallas_call(
        pair_kernel, in_specs=[VMEM] * 4, out_specs=HBM,
        out_shape=jax.ShapeDtypeStruct((NX, SUMS + TILE, LANES), BF16),
        scratch_shapes=[pltpu.VMEM((NX, SUMS + TILE, LANES), BF16), pltpu.SemaphoreType.DMA((NX,))],
        compiler_params=SMALL, name="pair",
    )(near(mine), near(base), near(rest), near(got))
    parts = lax.all_to_all(pair, "x", 0, 0, tiled=True)
    quad = pl.pallas_call(
        quad_kernel, in_specs=[VMEM], out_specs=VMEM, out_shape=pltpu.VMEM((QUAD, LANES), BF16),
        compiler_params=SMALL, name="quad",
    )(near(parts))
    both = lax.all_gather(quad, "zh", axis=0)
    group = NX * NY * NL
    total, squares = pl.pallas_call(
        total_kernel, in_specs=[VMEM] * 3, out_specs=[VMEM, HBM],
        out_shape=[pltpu.VMEM((GATHER, LANES), BF16), jax.ShapeDtypeStruct((group, 128), F32)],
        scratch_shapes=[pltpu.VMEM((group, 128), F32), pltpu.SemaphoreType.DMA],
        compiler_params=SMALL, name="total",
    )(near(both), near(momentum), near(theirs))
    shares = lax.all_to_all(squares, ("x", "y", "zl"), 0, 0, tiled=True)
    own = lax.all_gather(total, "x", axis=0)
    pack = pl.pallas_call(
        pack_kernel, in_specs=[VMEM] * 3, out_specs=VMEM, out_shape=pltpu.VMEM((PACK, LANES), BF16),
        compiler_params=SMALL, name="pack",
    )(near(shares), near(own), near(both))
    other = lax.ppermute(pack, "c", swap)
    entries = rows * width * NY * NL
    return pl.pallas_call(
        lambda *refs: final_kernel(entries, *refs),
        in_specs=[VMEM] * 4, out_specs=[HBM, HBM],
        out_shape=[jax.ShapeDtypeStruct((rows, width), BF16), jax.ShapeDtypeStruct(momentum.shape, F32)],
        scratch_shapes=[
            pltpu.VMEM((rows, width), BF16), pltpu.VMEM(momentum.shape, F32),
            pltpu.SemaphoreType.DMA((NX * NZ,)), pltpu.SemaphoreType.DMA,
        ],
        compiler_params=SMALL, name="final",
    )(near(global_weights), near(momentum), near(pack), near(other))


def solution(mesh):
    fine = Mesh(mesh.devices.reshape(NX, NZ, NC, NY, NL), AXES)
    in_specs = (P(REPLICA, FSDP, None), P(FSDP, None), P(FSDP, REPLICA))
    out_specs = (P(FSDP, None), P(FSDP, REPLICA))
    return jax.shard_map(
        per_device, mesh=fine, in_specs=in_specs, out_specs=out_specs, check_vma=False
    )
```

```python
import jax
import jax.numpy as jnp
from jax import lax
from jax.experimental import pallas as pl
from jax.experimental.pallas import tpu as pltpu
from jax.sharding import Mesh, PartitionSpec as P

NX, NZ, NC, NY, NL = 4, 2, 2, 8, 4
AXES = ("x", "zh", "c", "y", "zl")
REPLICA = ("x", "zh", "c")
FSDP = ("y", "zl")
REPLICAS = NX * NZ * NC
ROWS = 64
OWN = 512
LANES = 128
TILES = OWN // LANES
SUMS = NZ * TILES * ROWS
MOM = TILES * ROWS
TILE = 16
HALF = TILE // 2
MAIN = MOM - TILE
QUAD = SUMS + NX * HALF
LAST = SUMS + NZ * MAIN
GATHER = LAST + TILE
RESTS = NX * GATHER
SCALARS = RESTS + NZ * NX * HALF
PACK = SCALARS + 3 * TILE
F32, BF16 = jnp.float32, jnp.bfloat16
VMEM = pl.BlockSpec(memory_space=pltpu.VMEM)
HBM = pl.BlockSpec(memory_space=pl.ANY)
SMALL = pltpu.CompilerParams(vmem_limit_bytes=4 * 1024 * 1024)


def near(x):
    return pltpu.with_memory_space_constraint(x, pltpu.VMEM)


def far(x):
    return pltpu.with_memory_space_constraint(x, pltpu.HBM)


def flat(tile):
    return slice(tile * ROWS, (tile + 1) * ROWS)


def block_cols(x, h, core, t):
    return pl.ds(pl.multiple_of(((x * NZ + h) * NC + core) * OWN + t * LANES, LANES), LANES)


def fetch_kernel(local_ref, base_ref, mom_ref, local_out, base_out, rest_out, sems):
    core = lax.axis_index("c")
    copies = [
        pltpu.make_async_copy(
            mom_ref.at[ROWS - TILE:, OWN - LANES:], rest_out, sems.at[2 * NX * NZ]
        )
    ]
    for x in range(NX):
        for h in range(NZ):
            start = ((x * NZ + h) * NC + core) * OWN
            cols = pl.ds(pl.multiple_of(start, OWN), OWN)
            to = slice(h * OWN, (h + 1) * OWN)
            at = 2 * (x * NZ + h)
            copies.append(pltpu.make_async_copy(local_ref.at[0, :, cols], local_out.at[x, :, to], sems.at[at]))
            copies.append(pltpu.make_async_copy(base_ref.at[:, cols], base_out.at[x, :, to], sems.at[at + 1]))
    for copy in copies:
        copy.start()
    for copy in copies:
        copy.wait()


def fetch(local, base, momentum):
    half = pltpu.VMEM((NX, ROWS, NZ * OWN), BF16)
    return pl.pallas_call(
        fetch_kernel,
        in_specs=[HBM] * 3,
        out_specs=[VMEM] * 3,
        out_shape=[half, half, pltpu.VMEM((TILE, LANES), F32)],
        scratch_shapes=[pltpu.SemaphoreType.DMA((2 * NX * NZ + 1,))],
        cost_estimate=pl.CostEstimate(flops=0, bytes_accessed=2**22, transcendentals=0),
        compiler_params=SMALL,
        name="fetch",
    )(far(local), far(base), far(momentum))


def pair_kernel(local_ref, base_ref, rest_ref, got_ref, out_ref, buf, sems):
    core = lax.axis_index("c")
    copies = []
    for x in range(NX):
        for h in range(NZ):
            for t in range(TILES):
                cols = slice(h * OWN + t * LANES, h * OWN + (t + 1) * LANES)
                base = base_ref[x, :, cols].astype(F32)
                got = got_ref[0, :, block_cols(x, h, core, t)].astype(F32)
                pair = (local_ref[x, :, cols].astype(F32) - base) + (got - base)
                buf[x, flat(h * TILES + t), :] = pair.astype(BF16)
        buf[x, SUMS:, :] = rest_ref[...].astype(BF16)
        copies.append(pltpu.make_async_copy(buf.at[x], out_ref.at[x], sems.at[x]))
        copies[-1].start()
    for copy in copies:
        copy.wait()


def quad_kernel(parts_ref, out_ref):
    for t in range(NZ * TILES):
        total = parts_ref[0, flat(t), :].astype(F32)
        for k in range(1, NX):
            total = total + parts_ref[k, flat(t), :].astype(F32)
        out_ref[flat(t), :] = total.astype(BF16)
    for k in range(0, NX, 2):
        last = [parts_ref[k + i, SUMS:, :].astype(F32)[HALF:] for i in range(2)]
        at = SUMS + k * HALF
        out_ref[at:at + TILE, :] = jnp.concatenate(last, axis=0).astype(BF16)


def total_kernel(both_ref, mine_ref, theirs_ref, out_ref, squares_ref, buf, sem):
    acc = jnp.zeros((ROWS, LANES), F32)
    for t in range(NZ * TILES):
        total = both_ref[0, flat(t), :].astype(F32) + both_ref[1, flat(t), :].astype(F32)
        total = total.astype(BF16)
        out_ref[flat(t), :] = total
        acc = acc + total.astype(F32) * total.astype(F32)
    buf[...] = jnp.broadcast_to(jnp.sum(acc), buf.shape)
    copy = pltpu.make_async_copy(buf, squares_ref, sem)
    copy.start()
    half = lax.axis_index("zh")
    last = []
    for t in range(TILES):
        rows = ROWS - TILE if t == TILES - 1 else ROWS
        cols = slice(t * LANES, (t + 1) * LANES)
        mine, theirs = mine_ref[:, cols], theirs_ref[:, cols].astype(F32)
        for h in range(NZ):
            mom = jnp.where(half == h, mine, theirs)
            at = SUMS + h * MAIN + t * ROWS
            out_ref[at:at + rows, :] = mom[:rows].astype(BF16)
            if rows < ROWS:
                last.append(mom[rows:rows + HALF])
    out_ref[LAST:, :] = jnp.concatenate(last, axis=0).astype(BF16)
    copy.wait()


def pack_kernel(shares_ref, own_ref, both_ref, out_ref):
    for x in range(NX):
        out_ref[x * GATHER:(x + 1) * GATHER, :] = own_ref[x]
    for h in range(NZ):
        at = RESTS + h * NX * HALF
        out_ref[at:at + NX * HALF, :] = both_ref[h, SUMS:, :]
    left = jnp.broadcast_to(jnp.sum(shares_ref[:, 0:1]), (TILE, LANES))
    for k in range(3):
        part = left.astype(BF16)
        out_ref[SCALARS + k * TILE:SCALARS + (k + 1) * TILE, :] = part
        left = left - part.astype(F32)


def final_kernel(entries, base_ref, mom_ref, mine_ref, theirs_ref, new_ref, newmom_ref, buf, mom_buf, sems, mom_sem):
    core = lax.axis_index("c")
    squares = jnp.zeros((8, LANES), F32)
    for pack in (mine_ref, theirs_ref):
        parts = [pack[at:at + TILE, :].astype(F32)[:8] for at in range(SCALARS, PACK, TILE)]
        squares = squares + ((parts[2] + parts[1]) + parts[0])
    mean = squares / (REPLICAS * REPLICAS) / entries
    factor = jnp.minimum(1.0, 0.04 / jnp.sqrt(mean + 1e-06)) / REPLICAS
    sum_weight = (0.7 * 1.9) * factor

    def weights(rows, cols, total, mom):
        scaled = (total.astype(F32).reshape(-1, 8, LANES) * sum_weight[None]).reshape(-1, LANES)
        update = scaled + (0.7 * 0.81) * mom
        buf[rows, cols] = (base_ref[rows, cols].astype(F32) - update).astype(BF16)

    for t in range(TILES):
        at = lax.axis_index("x") * GATHER + (lax.axis_index("zh") * TILES + t) * ROWS
        total = mine_ref[pl.ds(pl.multiple_of(at, TILE), ROWS), :].astype(F32)
        cols = slice(t * LANES, (t + 1) * LANES)
        scaled = (total.reshape(-1, 8, LANES) * factor[None]).reshape(-1, LANES)
        mom_buf[:, cols] = 0.9 * mom_ref[:, cols] + scaled
    copies = [pltpu.make_async_copy(mom_buf, newmom_ref, mom_sem)]
    copies[0].start()
    for x in range(NX):
        for h in range(NZ):
            for which, pack in enumerate((mine_ref, theirs_ref)):
                owner = core if which == 0 else 1 - core
                for t in range(TILES):
                    cols = block_cols(x, h, owner, t)
                    at = x * GATHER + (h * TILES + t) * ROWS
                    mom_at = x * GATHER + SUMS + h * MAIN + t * ROWS
                    rows = ROWS - TILE if t == TILES - 1 else ROWS
                    mom = pack[mom_at:mom_at + rows, :].astype(F32)
                    weights(slice(0, rows), cols, pack[at:at + rows, :], mom)
                    if rows < ROWS:
                        last_at = x * GATHER + LAST
                        rest_at = RESTS + (h * NX + x) // 2 * TILE
                        last = pack[last_at:last_at + TILE, :].astype(F32)[h * HALF:(h + 1) * HALF]
                        rest = pack[rest_at:rest_at + TILE, :].astype(F32)[x % 2 * HALF:(x % 2 + 1) * HALF]
                        mom = jnp.concatenate([last, rest], axis=0)
                        weights(slice(rows, ROWS), cols, pack[at + rows:at + ROWS, :], mom)
                block = (x * NZ + h) * NC
                cols = pl.ds(pl.multiple_of((block + owner) * OWN, OWN), OWN)
                copies.append(pltpu.make_async_copy(buf.at[:, cols], new_ref.at[:, cols], sems.at[block + which]))
                copies[-1].start()
    for copy in copies:
        copy.wait()


def per_device(local_weights, global_weights, momentum):
    rows, width = global_weights.shape
    swap = [(0, 1), (1, 0)]
    theirs = lax.ppermute(momentum.astype(BF16), "zh", swap)
    got = lax.ppermute(local_weights, "c", swap)
    mine, base, rest = fetch(local_weights, global_weights, momentum)
    pair = pl.pallas_call(
        pair_kernel, in_specs=[VMEM] * 4, out_specs=HBM,
        out_shape=jax.ShapeDtypeStruct((NX, SUMS + TILE, LANES), BF16),
        scratch_shapes=[pltpu.VMEM((NX, SUMS + TILE, LANES), BF16), pltpu.SemaphoreType.DMA((NX,))],
        compiler_params=SMALL, name="pair",
    )(near(mine), near(base), near(rest), near(got))
    parts = lax.all_to_all(pair, "x", 0, 0, tiled=True)
    quad = pl.pallas_call(
        quad_kernel, in_specs=[VMEM], out_specs=VMEM, out_shape=pltpu.VMEM((QUAD, LANES), BF16),
        compiler_params=SMALL, name="quad",
    )(near(parts))
    both = lax.all_gather(quad, "zh", axis=0)
    group = NX * NY * NL
    total, squares = pl.pallas_call(
        total_kernel, in_specs=[VMEM] * 3, out_specs=[VMEM, HBM],
        out_shape=[pltpu.VMEM((GATHER, LANES), BF16), jax.ShapeDtypeStruct((group, 128), F32)],
        scratch_shapes=[pltpu.VMEM((group, 128), F32), pltpu.SemaphoreType.DMA],
        compiler_params=SMALL, name="total",
    )(near(both), near(momentum), near(theirs))
    shares = lax.all_to_all(squares, ("x", "y", "zl"), 0, 0, tiled=True)
    own = lax.all_gather(total, "x", axis=0)
    pack = pl.pallas_call(
        pack_kernel, in_specs=[VMEM] * 3, out_specs=VMEM, out_shape=pltpu.VMEM((PACK, LANES), BF16),
        compiler_params=SMALL, name="pack",
    )(near(shares), near(own), near(both))
    other = lax.ppermute(pack, "c", swap)
    entries = rows * width * NY * NL
    return pl.pallas_call(
        lambda *refs: final_kernel(entries, *refs),
        in_specs=[VMEM] * 4, out_specs=[HBM, HBM],
        out_shape=[jax.ShapeDtypeStruct((rows, width), BF16), jax.ShapeDtypeStruct(momentum.shape, F32)],
        scratch_shapes=[
            pltpu.VMEM((rows, width), BF16), pltpu.VMEM(momentum.shape, F32),
            pltpu.SemaphoreType.DMA((NX * NZ * NC,)), pltpu.SemaphoreType.DMA,
        ],
        compiler_params=SMALL, name="final",
    )(near(global_weights), near(momentum), near(pack), near(other))


def solution(mesh):
    fine = Mesh(mesh.devices.reshape(NX, NZ, NC, NY, NL), AXES)
    in_specs = (P(REPLICA, FSDP, None), P(FSDP, None), P(FSDP, REPLICA))
    out_specs = (P(FSDP, None), P(FSDP, REPLICA))
    return jax.shard_map(
        per_device, mesh=fine, in_specs=in_specs, out_specs=out_specs, check_vma=False
    )
```
